128 devices in a mesh: visit: 8 (over y, core), patch: 16 (over z, x).
Axes of the slice: x: 4, y: 4, z: 4, core: 2. Of those that a mesh axis runs over, the one named last changes fastest.
Arguments:
- image: float32 [4096, 128, 128], P(('visit', 'patch')), may hold values from -8 to 8
- weight: float32 [4096, 128, 128], P(('visit', 'patch')), may hold values from 0.25 to 4
- coeffs: float32 [4096, 16], P(('visit', 'patch')), may hold values from -3 to 3
- trim: int32 [4096, 4], P(('visit', 'patch')), may hold values from 0 to 31
- destination: int32 [4096], P(('visit', 'patch')), may hold values from 0 to 1023, as said below
- row_taps: float32 [16, 21], replicated, may hold values from -1 to 1
- col_taps: float32 [16, 21], replicated, may hold values from -1 to 1
Outputs:
- coadd: float32 [1024, 128, 128], P(('visit', 'patch'))
The draws below stay inside these ranges and needn't reach their ends.
Inputs may be any that keep to these rules, and one draw needn't show every extreme that they name: `destination`: entries n * 32 to (n + 1) * 32 - 1 belong to device n; of those, at most 5 name output tiles t of one column (t // 8) % 16, and on every device some column gets exactly 5.
All inputs are finite; a program needn't handle non-finite values.
Results may differ from the reference program's by a relative error of at most 0.00011.
Values sent between devices are 32-bit elements; how exact they have to be, the bound alone decides.
A program may use at most 128 MiB of HBM per device.

```python
import math
import jax
import jax.numpy as jnp
from jax import lax

TILE = 128
TAPS = 21
NB = 16
P_DEV = 32
TILES_DEV = 8
PATCH_COLUMNS = 16
COLUMN_TILES = 64
BLOCKS = 128
PIECES = 4096
OUT_TILES = 1024


def draw_destination(key, part):
    key = jax.random.fold_in(key, 7)
    hot_count = max(1, PATCH_COLUMNS // 4)
    half = P_DEV // 2

    def block(block_key):
        first, second, third = jax.random.split(block_key, 3)
        order = jax.random.permutation(first, PATCH_COLUMNS)
        index = jnp.arange(P_DEV, dtype=jnp.int32)
        pick = jnp.where(index < half, index % PATCH_COLUMNS, (index - half) % hot_count)
        column = order[pick]
        row_tile = jax.random.randint(second, (P_DEV,), 0, COLUMN_TILES)
        target = (row_tile // TILES_DEV * PATCH_COLUMNS + column) * TILES_DEV + row_tile % TILES_DEV
        return target[jax.random.permutation(third, P_DEV)]
    return jax.vmap(block)(jax.random.split(key, BLOCKS)).reshape(-1).astype(jnp.int32)


def plant(entries, rng, low, high):
    longest = entries.shape.index(max(entries.shape))
    spots = []
    for shift in (0, 1):
        where = [jax.random.randint(jax.random.fold_in(rng, axis), (), 0, length) for axis, length in enumerate(entries.shape)]
        where[longest] = (where[longest] + shift) % entries.shape[longest]
        spots.append(tuple(where))
    return entries.at[spots[0]].set(low).at[spots[1]].set(high)


def shard_levels(key, dims, pieces, low, largest):
    def one(dim, blocks):
        steps = jax.random.uniform(jax.random.fold_in(jax.random.fold_in(key, 6), dim), (blocks,), jnp.float32, low / len(pieces), largest / len(pieces))
        return jnp.repeat(jnp.exp(steps), dims[dim] // blocks).reshape((-1,) + (1,) * (len(dims) - dim - 1))

    level = one(*pieces[0])
    for cut in pieces[1:]:
        level = level * one(*cut)
    return level


def centred(key, extent, width, most, pieces=(), kind=jnp.bfloat16):
    array = jax.random.normal(key, extent, jnp.float32) * width
    if len(pieces) > 0:
        array = shard_levels(key, extent, pieces, -0.22, 0.18) * array
    return jnp.clip(array, min=-most, max=most).astype(kind)


def setup_inputs(seed: int = 0) -> dict:
    splits = jax.random.split(jax.random.key(seed), 8)
    return {
        "image": centred(splits[0], (PIECES, TILE, TILE), 1.0, 8.0, ((0, 128),), jnp.float32),
        "weight": jnp.clip(jnp.exp(math.log(4.0) - 2.7725887 * jax.random.uniform(splits[1], (PIECES, TILE, TILE), jnp.float32) ** shard_levels(splits[1], (PIECES, TILE, TILE), ((0, 128),), -0.2, 0.2)), 0.25, 4.0),
        "coeffs": centred(splits[2], (PIECES, NB), 0.5, 3.0, ((0, 128),), jnp.float32),
        "trim": plant(jax.random.randint(splits[3], (PIECES, 4), 0, TILE // 4), jax.random.fold_in(splits[3], 1), 0, (TILE // 4) - 1).astype(jnp.int32),
        "destination": draw_destination(jax.random.fold_in(splits[7], 71), 0),
        "row_taps": centred(splits[5], (NB, TAPS), 0.15, 1.0, (), jnp.float32),
        "col_taps": centred(splits[6], (NB, TAPS), 0.15, 1.0, (), jnp.float32),
    }


def match_tiles(image, coeffs, row_taps, col_taps):
    half = TAPS // 2

    def one(parts):
        tiles, weights = parts
        padded = jnp.pad(tiles, ((0, 0), (0, 0), (half, half)))
        result = jnp.zeros(tiles.shape, jnp.float32)
        for term in range(NB):
            across = jnp.zeros(tiles.shape, jnp.float32)
            for index in range(TAPS):
                across = across + col_taps[term, index] * padded[:, :, index:index + TILE]
            tall = jnp.pad(across, ((0, 0), (half, half), (0, 0)))
            down = jnp.zeros(tiles.shape, jnp.float32)
            for index in range(TAPS):
                down = down + row_taps[term, index] * tall[:, index:index + TILE, :]
            result = result + weights[:, term][:, None, None] * down
        return result

    blocks = image.shape[0] // P_DEV
    shaped = (image.reshape(blocks, P_DEV, TILE, TILE), coeffs.reshape(blocks, P_DEV, NB))
    return lax.map(one, shaped).reshape(image.shape)


def reference(image, weight, coeffs, trim, destination, row_taps, col_taps):
    matched = match_tiles(image, coeffs, row_taps, col_taps)
    pixel = jnp.arange(TILE, dtype=jnp.int32)
    rows_in = (pixel[None, :] >= trim[:, 0:1]) & (pixel[None, :] < TILE - trim[:, 1:2])
    cols_in = (pixel[None, :] >= trim[:, 2:3]) & (pixel[None, :] < TILE - trim[:, 3:4])
    inside = rows_in[:, :, None] & cols_in[:, None, :]
    kept = jnp.where(inside, weight, jnp.zeros_like(weight))
    numerator = jax.ops.segment_sum(kept * matched, destination, num_segments=OUT_TILES)
    denominator = jax.ops.segment_sum(kept, destination, num_segments=OUT_TILES)
    return numerator / (denominator + 1.0)
```

```python
import jax
import jax.numpy as jnp
from jax import lax
from jax.experimental import pallas as pl
from jax.experimental.pallas import tpu as pltpu
from jax.sharding import PartitionSpec as P

MESH = pl.DeviceIdType.MESH
F32 = jnp.float32
BF16 = jnp.bfloat16
I32 = jnp.int32

TILE = 128
TAPS = 21
NB = 16
COUNT = 32
OWNED = 8
SLOTS = 5
ROWS = 32
PARTS = TILE // ROWS
CHUNKS = 2 * PARTS
WINDOW = 80
QUAD = 4

SHIFTS = (
    (0, 0),
    (2, 2),
    (1, 2), (2, 1), (3, 2), (2, 3),
    (2, 0), (0, 2),
    (1, 1), (3, 3),
    (1, 3), (3, 1),
    (0, 1), (1, 0), (0, 3), (3, 0),
)
SIDE = 4
PLANE = len(SHIFTS)


def kernel(
    perm, dest, trim, coef, rtap, ctap, img, wgt, out,
    kept, nums, rl, cc, xr, wsp, send, recv, acc, msend, mrecv, tabv, tabs,
    csend, crecv, ysend, yrecv,
    s_sem, r_sem, ms_sem, mr_sem, cs_sem, cr_sem, ys_sem, yr_sem, tab_sem,
):
    visit, patch = lax.axis_index("visit"), lax.axis_index("patch")
    y, core = visit // 2, visit % 2
    z, x = patch // SIDE, patch % SIDE

    def column(d):
        dz, dx = SHIFTS[d]
        return lax.rem(z + dz, SIDE) * SIDE + lax.rem(x + dx, SIDE)

    def in_y(dy):
        return lax.rem(y + dy, SIDE) * 2 + core

    partners = [(visit, column(d)) for d in range(1, PLANE)]
    partners += [(visit + 1 - 2 * core, patch)]
    partners += [(in_y(dy), patch) for dy in range(1, SIDE)]
    barrier = pltpu.get_barrier_semaphore()
    for partner in partners:
        pl.semaphore_signal(barrier, inc=1, device_id=partner, device_id_type=MESH)

    row_of = lax.broadcasted_iota(I32, (TILE, TILE), 0)
    lane_of = lax.broadcasted_iota(I32, (TILE, TILE), 1)

    def keep(n, _):
        inside = (row_of >= trim[n, 0]) & (row_of < TILE - trim[n, 1])
        inside &= (lane_of >= trim[n, 2]) & (lane_of < TILE - trim[n, 3])
        kept[n] = jnp.where(inside, wgt[n], 0.0)
        return 0

    lax.fori_loop(0, COUNT, keep, 0)
    kept[COUNT] = jnp.zeros((TILE, TILE), F32)
    nums[COUNT] = jnp.zeros((TILE, TILE), F32)

    sub_of = lax.broadcasted_iota(I32, (8, TILE), 0)

    def meta_copy(d):
        return pltpu.make_async_remote_copy(
            src_ref=msend.at[d], dst_ref=mrecv.at[d],
            send_sem=ms_sem.at[d], recv_sem=mr_sem.at[d],
            device_id=(visit, column(d)), device_id_type=MESH,
        )

    def plane_copy(c, d):
        return pltpu.make_async_remote_copy(
            src_ref=send.at[c, d], dst_ref=recv.at[c, d],
            send_sem=s_sem.at[c, d], recv_sem=r_sem.at[c, d],
            device_id=(visit, column(d)), device_id_type=MESH,
        )

    def plane_wait(c, d):
        return pltpu.make_async_remote_copy(
            src_ref=send.at[c, d], dst_ref=recv.at[c, d],
            send_sem=s_sem.at[c, d], recv_sem=r_sem.at[c, d],
            device_id=(visit, column(1)), device_id_type=MESH,
        )

    def core_copy(c):
        return pltpu.make_async_remote_copy(
            src_ref=csend.at[c], dst_ref=crecv.at[c],
            send_sem=cs_sem.at[c], recv_sem=cr_sem.at[c],
            device_id=(visit + 1 - 2 * core, patch), device_id_type=MESH,
        )

    def y_copy(c, dy):
        return pltpu.make_async_remote_copy(
            src_ref=ysend.at[c, dy], dst_ref=yrecv.at[c, dy],
            send_sem=ys_sem.at[c, dy], recv_sem=yr_sem.at[c, dy],
            device_id=(in_y(dy), patch), device_id_type=MESH,
        )

    for d in range(PLANE):
        rows = jnp.full((8, TILE), -1, I32)
        for k in range(SLOTS):
            n = perm[column(d) * 8 + k]
            to = dest[jnp.minimum(n, COUNT - 1)]
            row = jnp.where(n < COUNT, to // (OWNED * PLANE) * OWNED + to % OWNED, -1)
            rows = jnp.where(sub_of == k, row, rows)
        if d == 0:
            mrecv[0] = rows
        else:
            msend[d] = rows

    def fill(source, c, q, d):
        for k in range(SLOTS):
            n = perm[column(d) * 8 + k]
            block = source[n, pl.ds(q * ROWS, ROWS), :]
            target = recv if d == 0 else send
            target[c, d, k * ROWS:(k + 1) * ROWS, :] = block

    def send_part(source, first):
        def one(q, _):
            c = first + q
            for d in range(1, PLANE):
                fill(source, c, q, d)
                plane_copy(c, d).start()
            fill(source, c, q, 0)
            return 0

        return one

    pl.semaphore_wait(barrier, len(partners))
    for d in range(1, PLANE):
        meta_copy(d).start()
    lax.fori_loop(0, PARTS, send_part(kept, 0), 0)

    half_row = lax.broadcasted_iota(I32, (TILE // 2, 2 * TILE), 0)
    half_lane = lax.broadcasted_iota(I32, (TILE // 2, 2 * TILE), 1)
    piece = (half_lane >= WINDOW).astype(I32) + (half_lane >= 2 * WINDOW).astype(I32)
    place = half_lane - piece * WINDOW

    def tables(k, _):
        for h in range(2):
            offset = place + h * (TILE - WINDOW) - half_row - h * (TILE // 2) + TAPS // 2
            offset = jnp.where(half_lane < 3 * WINDOW, offset, -1)
            taps = jnp.zeros((TILE // 2, 2 * TILE), F32)
            for index in range(TAPS):
                taps = jnp.where(offset == index, rtap[k, index], taps)
            high = taps.astype(BF16).astype(F32)
            rl[h, pl.ds(k * (TILE // 2), TILE // 2), :] = jnp.where(
                piece == 2, taps - high, high
            ).astype(BF16)
        offset = row_of - lane_of + TAPS // 2
        taps = jnp.zeros((TILE, TILE), F32)
        for index in range(TAPS):
            taps = jnp.where(offset == index, ctap[k, index], taps)
        high = taps.astype(BF16)
        cc[pl.ds(k * TILE, TILE), 0:TILE] = high
        cc[pl.ds(k * TILE, TILE), TILE:] = (taps - high.astype(F32)).astype(BF16)
        return 0

    lax.fori_loop(0, NB, tables, 0)
    for h in range(2):
        xr[h, 3 * WINDOW:, :] = jnp.zeros((2 * TILE - 3 * WINDOW, 2 * TILE), BF16)

    def match(i, _):
        for pair in range(QUAD // 2):
            for u in range(2):
                pixels = img[i * QUAD + pair * 2 + u]
                high = pixels.astype(BF16)
                low = (pixels - high.astype(F32)).astype(BF16)
                lanes = slice(u * TILE, (u + 1) * TILE)
                for h in range(2):
                    a = h * (TILE - WINDOW)
                    xr[h, 0:WINDOW, lanes] = high[a:a + WINDOW]
                    xr[h, WINDOW:2 * WINDOW, lanes] = low[a:a + WINDOW]
                    xr[h, 2 * WINDOW:3 * WINDOW, lanes] = high[a:a + WINDOW]
            for h in range(2):
                for g in range(0, NB, 4):
                    down = jnp.dot(
                        rl[h, g * (TILE // 2):(g + 4) * (TILE // 2), :], xr[h],
                        preferred_element_type=F32,
                    )
                    for k in range(g, g + 4):
                        for u in range(2):
                            t = pair * 2 + u
                            b = (k - g) * (TILE // 2)
                            w = down[b:b + TILE // 2, u * TILE:(u + 1) * TILE]
                            w = w * coef[i * QUAD + t, k]
                            high = w.astype(BF16)
                            r = t * TILE + h * (TILE // 2)
                            lanes = slice(k * TILE, (k + 1) * TILE)
                            wsp[r:r + TILE // 2, lanes] = high
                            r += QUAD * TILE
                            wsp[r:r + TILE // 2, lanes] = (w - high.astype(F32)).astype(BF16)
        both = jnp.dot(wsp[...], cc[...], preferred_element_type=F32)
        both = both[:, :TILE] + both[:, TILE:]
        for t in range(QUAD):
            n = i * QUAD + t
            matched = both[t * TILE:(t + 1) * TILE]
            matched = matched + both[(QUAD + t) * TILE:(QUAD + t + 1) * TILE]
            nums[n] = kept[n] * matched
        return 0

    lax.fori_loop(0, COUNT // QUAD, match, 0)
    lax.fori_loop(0, PARTS, send_part(nums, PARTS), 0)

    for d in range(1, PLANE):
        meta_copy(d).wait_recv()
    along = mrecv[...].reshape(TILE, TILE)
    across = along.T
    before = jnp.where((along == across) & (row_of < lane_of), row_of, -1)
    before = jnp.max(before, axis=0, keepdims=True)
    last = jnp.max(jnp.where(along == lane_of, row_of, -1), axis=0, keepdims=True)
    table = jnp.where(sub_of == 0, before, last)
    tabv[...] = jnp.where(table < 0, TILE, table)
    move = pltpu.make_async_copy(tabv, tabs, tab_sem)
    move.start()
    move.wait()
    acc[TILE] = jnp.zeros((ROWS, TILE), F32)

    def entry(r, s):
        return jnp.clip(tabs[r, s], 0, TILE)

    def gather(c):
        def add(d):
            for k in range(SLOTS):
                s = d * 8 + k
                acc[s] = recv[c, d, k * ROWS:(k + 1) * ROWS, :] + acc[entry(0, s)]

        def one(d, _):
            plane_wait(c, d).wait_recv()
            add(d)
            return 0

        add(0)
        lax.fori_loop(1, PLANE, one, 0)
        for dy in range(SIDE):
            group = lax.rem(y + dy, SIDE) * 2
            for j in range(OWNED):
                other = entry(1, (group + 1 - core) * OWNED + j)
                csend[c, dy, j] = acc[other]
        core_copy(c).start()
        for dy in range(SIDE):
            group = lax.rem(y + dy, SIDE) * 2
            for j in range(OWNED):
                ysend[c, dy, j] = acc[entry(1, (group + core) * OWNED + j)]

    def spread(c):
        core_copy(c).wait_recv()
        for dy in (2, 1, 3, 0):
            ysend[c, dy] = ysend[c, dy] + crecv[c, dy]
            if dy:
                y_copy(c, dy).start()

    def total(c):
        for dy in range(1, SIDE):
            y_copy(c, dy).wait_recv()
        return (ysend[c, 0] + yrecv[c, 1]) + (yrecv[c, 2] + yrecv[c, 3])

    def weights(q, _):
        gather(q)
        spread(q)
        return 0

    lax.fori_loop(0, PARTS, weights, 0)

    def finish(q, _):
        value = total(PARTS + q) / (total(q) + 1.0)
        for j in range(OWNED):
            out[j, pl.ds(q * ROWS, ROWS), :] = value[j]
        return 0

    def pixels(q, _):
        gather(PARTS + q)
        spread(PARTS + q)
        return 0

    lax.fori_loop(0, PARTS, pixels, 0)
    lax.fori_loop(0, PARTS, finish, 0)

    def drain(c, _):
        def one(d, _):
            plane_wait(c, d).wait_send()
            return 0

        lax.fori_loop(1, PLANE, one, 0)
        core_copy(c).wait_send()
        for dy in range(1, SIDE):
            y_copy(c, dy).wait_send()
        return 0

    lax.fori_loop(0, CHUNKS, drain, 0)
    for d in range(1, PLANE):
        meta_copy(d).wait_send()


def shards(image, weight, coeffs, trim, destination, row_taps, col_taps):
    column = destination // OWNED % PLANE
    order = jnp.arange(COUNT, dtype=I32)
    earlier = (column[:, None] == column[None, :]) & (order[None, :] < order[:, None])
    slot = column * 8 + jnp.sum(earlier.astype(I32), axis=1)
    match = jnp.arange(PLANE * 8, dtype=I32)[:, None] == slot[None, :]
    perm = jnp.min(jnp.where(match, order[None, :], COUNT), axis=1)
    smem = pl.BlockSpec(memory_space=pltpu.SMEM)
    vmem = pl.BlockSpec(memory_space=pltpu.VMEM)
    dma = pltpu.SemaphoreType.DMA
    return pl.pallas_call(
        kernel,
        out_shape=jax.ShapeDtypeStruct((OWNED, TILE, TILE), F32),
        in_specs=[smem] * 6 + [vmem] * 2,
        out_specs=vmem,
        scratch_shapes=[
            pltpu.VMEM((COUNT + 1, TILE, TILE), F32),
            pltpu.VMEM((COUNT + 1, TILE, TILE), F32),
            pltpu.VMEM((2, NB * TILE // 2, 2 * TILE), BF16),
            pltpu.VMEM((NB * TILE, 2 * TILE), BF16),
            pltpu.VMEM((2, 2 * TILE, 2 * TILE), BF16),
            pltpu.VMEM((2 * QUAD * TILE, NB * TILE), BF16),
            pltpu.VMEM((CHUNKS, PLANE, SLOTS * ROWS, TILE), F32),
            pltpu.VMEM((CHUNKS, PLANE, SLOTS * ROWS, TILE), F32),
            pltpu.VMEM((TILE + 1, ROWS, TILE), F32),
            pltpu.VMEM((PLANE, 8, TILE), I32),
            pltpu.VMEM((PLANE, 8, TILE), I32),
            pltpu.VMEM((8, TILE), I32),
            pltpu.SMEM((8, TILE), I32),
            pltpu.VMEM((CHUNKS, SIDE, OWNED, ROWS, TILE), F32),
            pltpu.VMEM((CHUNKS, SIDE, OWNED, ROWS, TILE), F32),
            pltpu.VMEM((CHUNKS, SIDE, OWNED, ROWS, TILE), F32),
            pltpu.VMEM((CHUNKS, SIDE, OWNED, ROWS, TILE), F32),
            dma((CHUNKS, PLANE)),
            dma((CHUNKS, PLANE)),
            dma((PLANE,)),
            dma((PLANE,)),
            dma((CHUNKS,)),
            dma((CHUNKS,)),
            dma((CHUNKS, SIDE)),
            dma((CHUNKS, SIDE)),
            dma(()),
        ],
        compiler_params=pltpu.CompilerParams(
            collective_id=0, has_side_effects=True, vmem_limit_bytes=60 << 20
        ),
        name="coadd",
    )(perm, destination, trim, coeffs, row_taps, col_taps, image, weight)


def solution(mesh):
    placed = (
        P(("visit", "patch"), None, None),
        P(("visit", "patch"), None, None),
        P(("visit", "patch"), None),
        P(("visit", "patch"), None),
        P(("visit", "patch")),
        P(),
        P(),
    )
    return jax.shard_map(
        shards,
        mesh=mesh,
        in_specs=placed,
        out_specs=P(("visit", "patch"), None, None),
        check_vma=False,
    )
```

```python
import jax
import jax.numpy as jnp
from jax import lax
from jax.experimental import pallas as pl
from jax.experimental.pallas import tpu as pltpu
from jax.sharding import PartitionSpec as P

MESH = pl.DeviceIdType.MESH
F32 = jnp.float32
BF16 = jnp.bfloat16
I32 = jnp.int32

TILE = 128
TAPS = 21
NB = 16
COUNT = 32
OWNED = 8
SLOTS = 5
WINDOW = 80
QUAD = 4

WEIGHT_GROUPS = ((0, 32, 4),)
PIXEL_GROUPS = ((0, 32, 3), (96, 16, 1), (112, 8, 2))
WEIGHT_CHUNKS = sum(g[2] for g in WEIGHT_GROUPS)
CHUNKS = WEIGHT_CHUNKS + sum(g[2] for g in PIXEL_GROUPS)
MOST = 32

SHIFTS = (
    (0, 0),
    (2, 2),
    (1, 2), (2, 1), (3, 2), (2, 3),
    (2, 0), (0, 2),
    (1, 1), (3, 3),
    (1, 3), (3, 1),
    (0, 1), (1, 0), (0, 3), (3, 0),
)
SIDE = 4
PLANE = len(SHIFTS)
Y_ORDER = (2, 1, 3, 0)


class Chunk:
    def __init__(self, c, start, rows, base):
        self.c, self.start, self.rows = c, start, rows
        self.at = base + start

    def slots(self, d):
        return d, pl.ds(pl.multiple_of(self.at * SLOTS, 8), self.rows * SLOTS), slice(None)

    def slot(self, d, k):
        return d, pl.ds(pl.multiple_of(self.at * SLOTS + k * self.rows, 8), self.rows), slice(None)

    def eight(self, dy):
        first = self.at * SIDE * OWNED + dy * OWNED * self.rows
        return pl.ds(pl.multiple_of(first, 8), OWNED * self.rows), slice(None)

    def one(self, dy, j):
        first = self.at * SIDE * OWNED + (dy * OWNED + j) * self.rows
        return pl.ds(pl.multiple_of(first, 8), self.rows), slice(None)


def kernel(
    dest, trim, coef, rtap, ctap, img_hbm, wgt_hbm, out_hbm,
    img, wgt, res, kept, nums, rl, cc, xr, wsp, send, recv, acc, msend, mrecv,
    permv, perms, tabv, tabs, csend, crecv, ysend, yrecv,
    i_sem, w_sem, o_sem, s_sem, r_sem, ms_sem, mr_sem, cs_sem, cr_sem, ys_sem, yr_sem, t_sem,
):
    visit, patch = lax.axis_index("visit"), lax.axis_index("patch")
    y, core = visit // 2, visit % 2
    z, x = patch // SIDE, patch % SIDE

    def column(d):
        dz, dx = SHIFTS[d]
        return lax.rem(z + dz, SIDE) * SIDE + lax.rem(x + dx, SIDE)

    def in_y(dy):
        return lax.rem(y + dy, SIDE) * 2 + core

    load_weight = pltpu.make_async_copy(wgt_hbm, wgt, w_sem)
    load_weight.start()
    load_image = pltpu.make_async_copy(img_hbm, img, i_sem)
    load_image.start()

    partners = [(visit, column(d)) for d in range(1, PLANE)]
    partners += [(visit + 1 - 2 * core, patch)]
    partners += [(in_y(dy), patch) for dy in range(1, SIDE)]
    barrier = pltpu.get_barrier_semaphore()
    for partner in partners:
        pl.semaphore_signal(barrier, inc=1, device_id=partner, device_id_type=MESH)

    row_of = lax.broadcasted_iota(I32, (TILE, TILE), 0)
    lane_of = lax.broadcasted_iota(I32, (TILE, TILE), 1)
    sub_of = lax.broadcasted_iota(I32, (8, TILE), 0)

    rows_c, lanes_c = row_of[:COUNT], lane_of[:COUNT]
    by_row = jnp.zeros((COUNT, TILE), I32)
    by_lane = jnp.full((COUNT, TILE), -1, I32)
    for n in range(COUNT):
        place = dest[n] // OWNED % PLANE
        by_row = jnp.where(rows_c == n, place, by_row)
        by_lane = jnp.where(lanes_c == n, place, by_lane)
    earlier = (by_row == by_lane) & (lanes_c < rows_c)
    rank = jnp.sum(earlier.astype(I32), axis=1, keepdims=True)
    tile_of = jnp.where(by_row * 8 + rank == lanes_c, rows_c, COUNT)
    permv[...] = jnp.broadcast_to(jnp.min(tile_of, axis=0, keepdims=True), (8, TILE))
    move = pltpu.make_async_copy(permv, perms, t_sem)
    move.start()

    load_weight.wait()

    def keep(n, _):
        inside = (row_of >= trim[0, n]) & (row_of < TILE - trim[1, n])
        inside &= (lane_of >= trim[2, n]) & (lane_of < TILE - trim[3, n])
        kept[n] = jnp.where(inside, wgt[n], 0.0)
        return 0

    lax.fori_loop(0, COUNT, keep, 0)
    kept[COUNT] = jnp.zeros((TILE, TILE), F32)
    nums[COUNT] = jnp.zeros((TILE, TILE), F32)
    move.wait()

    def tile_in(d, k):
        return jnp.clip(perms[0, column(d) * 8 + k], 0, COUNT)

    def remote(src, dst, send_sem, recv_sem, to):
        return pltpu.make_async_remote_copy(
            src_ref=src, dst_ref=dst, send_sem=send_sem, recv_sem=recv_sem,
            device_id=to, device_id_type=MESH,
        )

    def meta_copy(d):
        return remote(msend.at[d], mrecv.at[d], ms_sem.at[d], mr_sem.at[d], (visit, column(d)))

    def plane_copy(chunk, d, to):
        part = chunk.slots(d)
        c = chunk.c
        return remote(send.at[part], recv.at[part], s_sem.at[c, d], r_sem.at[c, d], (visit, to))

    def core_copy(chunk, dy):
        part = chunk.eight(dy)
        to = (visit + 1 - 2 * core, patch)
        c = chunk.c
        return remote(csend.at[part], crecv.at[part], cs_sem.at[c, dy], cr_sem.at[c, dy], to)

    def y_copy(chunk, dy):
        part = chunk.eight(dy)
        c = chunk.c
        to = (in_y(dy), patch)
        return remote(ysend.at[part], yrecv.at[part], ys_sem.at[c, dy], yr_sem.at[c, dy], to)

    def fill(source, chunk, d):
        target = recv if d == 0 else send
        for k in range(SLOTS):
            block = source[tile_in(d, k), pl.ds(chunk.start, chunk.rows), :]
            target[chunk.slot(d, k)] = block

    def send_chunk(source, chunk):
        for d in range(1, PLANE):
            fill(source, chunk, d)
            plane_copy(chunk, d, column(d)).start()
        fill(source, chunk, 0)

    def loop(groups, c, base, first, body):
        for start, rows, count in groups:

            def one(q, _, start=start, rows=rows, c=c):
                body(Chunk(c + q, start + q * rows, rows, base))
                return 0

            begin = min(first, count)
            lax.fori_loop(begin, count, one, 0)
            first -= begin
            c += count

    weight_args = (WEIGHT_GROUPS, 0, 0)
    pixel_args = (PIXEL_GROUPS, WEIGHT_CHUNKS, TILE)

    pl.semaphore_wait(barrier, len(partners))
    send_chunk(kept, Chunk(0, 0, WEIGHT_GROUPS[0][1], 0))
    for d in range(PLANE):
        rows = jnp.full((8, TILE), -1, I32)
        for k in range(SLOTS):
            n = tile_in(d, k)
            to = dest[jnp.minimum(n, COUNT - 1)]
            row = jnp.where(n < COUNT, to // (OWNED * PLANE) * OWNED + to % OWNED, -1)
            rows = jnp.where(sub_of == k, row, rows)
        if d == 0:
            mrecv[0] = rows
        else:
            msend[d] = rows
            meta_copy(d).start()
    loop(*weight_args, 1, lambda chunk: send_chunk(kept, chunk))

    half_row = lax.broadcasted_iota(I32, (TILE // 2, 2 * TILE), 0)
    half_lane = lax.broadcasted_iota(I32, (TILE // 2, 2 * TILE), 1)
    piece = (half_lane >= WINDOW).astype(I32) + (half_lane >= 2 * WINDOW).astype(I32)
    place = half_lane - piece * WINDOW

    def tables(k, _):
        for h in range(2):
            offset = place + h * (TILE - WINDOW) - half_row - h * (TILE // 2) + TAPS // 2
            offset = jnp.where(half_lane < 3 * WINDOW, offset, -1)
            taps = jnp.zeros((TILE // 2, 2 * TILE), F32)
            for index in range(TAPS):
                taps = jnp.where(offset == index, rtap[k, index], taps)
            high = taps.astype(BF16).astype(F32)
            rl[h, pl.ds(k * (TILE // 2), TILE // 2), :] = jnp.where(
                piece == 2, taps - high, high
            ).astype(BF16)
        offset = row_of - lane_of + TAPS // 2
        taps = jnp.zeros((TILE, TILE), F32)
        for index in range(TAPS):
            taps = jnp.where(offset == index, ctap[k, index], taps)
        high = taps.astype(BF16)
        cc[pl.ds(k * TILE, TILE), 0:TILE] = high
        cc[pl.ds(k * TILE, TILE), TILE:] = (taps - high.astype(F32)).astype(BF16)
        return 0

    lax.fori_loop(0, NB, tables, 0)
    load_image.wait()
    for h in range(2):
        xr[h, 3 * WINDOW:, :] = jnp.zeros((2 * TILE - 3 * WINDOW, 2 * TILE), BF16)

    def match(i, _):
        for pair in range(QUAD // 2):
            for u in range(2):
                pixels = img[i * QUAD + pair * 2 + u]
                high = pixels.astype(BF16)
                low = (pixels - high.astype(F32)).astype(BF16)
                lanes = slice(u * TILE, (u + 1) * TILE)
                for h in range(2):
                    a = h * (TILE - WINDOW)
                    xr[h, 0:WINDOW, lanes] = high[a:a + WINDOW]
                    xr[h, WINDOW:2 * WINDOW, lanes] = low[a:a + WINDOW]
                    xr[h, 2 * WINDOW:3 * WINDOW, lanes] = high[a:a + WINDOW]
            for h in range(2):
                for g in range(0, NB, 4):
                    down = jnp.dot(
                        rl[h, g * (TILE // 2):(g + 4) * (TILE // 2), :], xr[h],
                        preferred_element_type=F32,
                    )
                    for k in range(g, g + 4):
                        for u in range(2):
                            t = pair * 2 + u
                            b = (k - g) * (TILE // 2)
                            w = down[b:b + TILE // 2, u * TILE:(u + 1) * TILE]
                            w = w * coef[k, i * QUAD + t]
                            high = w.astype(BF16)
                            r = t * TILE + h * (TILE // 2)
                            lanes = slice(k * TILE, (k + 1) * TILE)
                            wsp[r:r + TILE // 2, lanes] = high
                            r += QUAD * TILE
                            wsp[r:r + TILE // 2, lanes] = (w - high.astype(F32)).astype(BF16)
        both = jnp.dot(wsp[...], cc[...], preferred_element_type=F32)
        both = both[:, :TILE] + both[:, TILE:]
        for t in range(QUAD):
            n = i * QUAD + t
            matched = both[t * TILE:(t + 1) * TILE]
            matched = matched + both[(QUAD + t) * TILE:(QUAD + t + 1) * TILE]
            nums[n] = kept[n] * matched
        return 0

    lax.fori_loop(0, COUNT // QUAD, match, 0)
    loop(*pixel_args, 0, lambda chunk: send_chunk(nums, chunk))

    for d in range(1, PLANE):
        meta_copy(d).wait()
    along = mrecv[...].reshape(TILE, TILE)
    across = along.T
    before = jnp.where((along == across) & (row_of < lane_of), row_of, -1)
    before = jnp.max(before, axis=0, keepdims=True)
    last = jnp.max(jnp.where(along == lane_of, row_of, -1), axis=0, keepdims=True)
    table = jnp.where(sub_of == 0, before, last)
    tabv[...] = jnp.where(table < 0, TILE, table)
    move = pltpu.make_async_copy(tabv, tabs, t_sem)
    move.start()
    move.wait()
    acc[TILE] = jnp.zeros((MOST, TILE), F32)

    def entry(r, s):
        return jnp.clip(tabs[r, s], 0, TILE)

    def gather(chunk):
        rows = chunk.rows

        def add(d):
            for k in range(SLOTS):
                s = d * 8 + k
                acc[s, :rows] = recv[chunk.slot(d, k)] + acc[entry(0, s), :rows]

        def one(d, _):
            plane_copy(chunk, d, column(1)).wait_recv()
            add(d)
            return 0

        add(0)
        lax.fori_loop(1, PLANE, one, 0)
        for dy in Y_ORDER:
            group = lax.rem(y + dy, SIDE) * 2
            for j in range(OWNED):
                csend[chunk.one(dy, j)] = acc[entry(1, (group + 1 - core) * OWNED + j), :rows]
            core_copy(chunk, dy).start()
        for dy in Y_ORDER:
            group = lax.rem(y + dy, SIDE) * 2
            for j in range(OWNED):
                ysend[chunk.one(dy, j)] = acc[entry(1, (group + core) * OWNED + j), :rows]

    def spread(chunk):
        for dy in Y_ORDER:
            part = chunk.eight(dy)
            core_copy(chunk, dy).wait_recv()
            ysend[part] = ysend[part] + crecv[part]
            if dy:
                y_copy(chunk, dy).start()

    def drain(chunk):
        def one(d, _):
            plane_copy(chunk, d, column(1)).wait_send()
            return 0

        lax.fori_loop(1, PLANE, one, 0)
        for dy in range(SIDE):
            core_copy(chunk, dy).wait_send()
            if dy:
                y_copy(chunk, dy).wait_send()

    def total(chunk):
        for dy in range(1, SIDE):
            y_copy(chunk, dy).wait_recv()
        a, b, c, d = (chunk.eight(dy) for dy in range(SIDE))
        return (ysend[a] + yrecv[b]) + (yrecv[c] + yrecv[d])

    def weights(chunk):
        gather(chunk)
        spread(chunk)

    def sums(chunk):
        value = total(chunk) + 1.0
        for j in range(OWNED):
            block = value[j * chunk.rows:(j + 1) * chunk.rows]
            res[j, pl.ds(chunk.start, chunk.rows), :] = block

    def finish(chunk):
        value = total(chunk)
        for j in range(OWNED):
            part = (j, pl.ds(chunk.start, chunk.rows), slice(None))
            res[part] = value[j * chunk.rows:(j + 1) * chunk.rows] / res[part]

    def store(chunk):
        part = (slice(None), pl.ds(chunk.start, chunk.rows), slice(None))
        return pltpu.make_async_copy(res.at[part], out_hbm.at[part], o_sem.at[chunk.c])

    loop(*weight_args, 0, weights)
    loop(*weight_args, 0, sums)
    loop(*weight_args, 0, drain)

    pixel_chunks = []
    c = WEIGHT_CHUNKS
    for start, rows, count in PIXEL_GROUPS:
        for q in range(count):
            pixel_chunks.append(Chunk(c, start + q * rows, rows, TILE))
            c += 1
    for index, chunk in enumerate(pixel_chunks):
        gather(chunk)
        spread(chunk)
        if index:
            finish(pixel_chunks[index - 1])
            store(pixel_chunks[index - 1]).start()
        if index > 1:
            drain(pixel_chunks[index - 2])
    finish(pixel_chunks[-1])
    store(pixel_chunks[-1]).start()
    for chunk in pixel_chunks[-2:]:
        drain(chunk)
    for chunk in pixel_chunks:
        store(chunk).wait()


def shards(image, weight, coeffs, trim, destination, row_taps, col_taps):
    smem = pl.BlockSpec(memory_space=pltpu.SMEM)
    hbm = pl.BlockSpec(memory_space=pl.ANY)
    dma = pltpu.SemaphoreType.DMA
    stack = 2 * TILE * SIDE * OWNED
    return pl.pallas_call(
        kernel,
        out_shape=jax.ShapeDtypeStruct((OWNED, TILE, TILE), F32),
        in_specs=[smem] * 5 + [hbm] * 2,
        out_specs=hbm,
        scratch_shapes=[
            pltpu.VMEM((COUNT, TILE, TILE), F32),
            pltpu.VMEM((COUNT, TILE, TILE), F32),
            pltpu.VMEM((OWNED, TILE, TILE), F32),
            pltpu.VMEM((COUNT + 1, TILE, TILE), F32),
            pltpu.VMEM((COUNT + 1, TILE, TILE), F32),
            pltpu.VMEM((2, NB * TILE // 2, 2 * TILE), BF16),
            pltpu.VMEM((NB * TILE, 2 * TILE), BF16),
            pltpu.VMEM((2, 2 * TILE, 2 * TILE), BF16),
            pltpu.VMEM((2 * QUAD * TILE, NB * TILE), BF16),
            pltpu.VMEM((PLANE, 2 * TILE * SLOTS, TILE), F32),
            pltpu.VMEM((PLANE, 2 * TILE * SLOTS, TILE), F32),
            pltpu.VMEM((TILE + 1, MOST, TILE), F32),
            pltpu.VMEM((PLANE, 8, TILE), I32),
            pltpu.VMEM((PLANE, 8, TILE), I32),
            pltpu.VMEM((8, TILE), I32),
            pltpu.SMEM((8, TILE), I32),
            pltpu.VMEM((8, TILE), I32),
            pltpu.SMEM((8, TILE), I32),
            pltpu.VMEM((stack, TILE), F32),
            pltpu.VMEM((stack, TILE), F32),
            pltpu.VMEM((stack, TILE), F32),
            pltpu.VMEM((stack, TILE), F32),
            dma(()),
            dma(()),
            dma((CHUNKS,)),
            dma((CHUNKS, PLANE)),
            dma((CHUNKS, PLANE)),
            dma((PLANE,)),
            dma((PLANE,)),
            dma((CHUNKS, SIDE)),
            dma((CHUNKS, SIDE)),
            dma((CHUNKS, SIDE)),
            dma((CHUNKS, SIDE)),
            dma(()),
        ],
        compiler_params=pltpu.CompilerParams(
            collective_id=0, has_side_effects=True, vmem_limit_bytes=60 << 20
        ),
        name="coadd",
    )(destination, trim.T, coeffs.T, row_taps, col_taps, image, weight)


def solution(mesh):
    placed = (
        P(("visit", "patch"), None, None),
        P(("visit", "patch"), None, None),
        P(("visit", "patch"), None),
        P(("visit", "patch"), None),
        P(("visit", "patch")),
        P(),
        P(),
    )
    return jax.shard_map(
        shards,
        mesh=mesh,
        in_specs=placed,
        out_specs=P(("visit", "patch"), None, None),
        check_vma=False,
    )
```

```python
import jax
import jax.numpy as jnp
from jax import lax
from jax.experimental import pallas as pl
from jax.experimental.pallas import tpu as pltpu
from jax.sharding import PartitionSpec as P

MESH = pl.DeviceIdType.MESH
F32 = jnp.float32
BF16 = jnp.bfloat16
I32 = jnp.int32

TILE = 128
TAPS = 21
NB = 16
COUNT = 32
OWNED = 8
SLOTS = 5
WINDOW = 80
QUAD = 4

WEIGHT_GROUPS = ((0, 32, 4),)
PIXEL_GROUPS = ((0, 32, 3), (96, 16, 1), (112, 8, 2))
WEIGHT_CHUNKS = sum(g[2] for g in WEIGHT_GROUPS)
CHUNKS = WEIGHT_CHUNKS + sum(g[2] for g in PIXEL_GROUPS)
MOST = 32

SHIFTS = (
    (0, 0),
    (2, 2),
    (1, 2), (2, 1), (3, 2), (2, 3),
    (2, 0), (0, 2),
    (1, 1), (3, 3),
    (1, 3), (3, 1),
    (0, 1), (1, 0), (0, 3), (3, 0),
)
SIDE = 4
PLANE = len(SHIFTS)
Y_ORDER = (2, 1, 3, 0)


class Chunk:
    def __init__(self, c, start, rows, base):
        self.c, self.start, self.rows = c, start, rows
        self.at = base + start

    def slots(self, d):
        return d, pl.ds(pl.multiple_of(self.at * SLOTS, 8), self.rows * SLOTS), slice(None)

    def slot(self, d, k):
        return d, pl.ds(pl.multiple_of(self.at * SLOTS + k * self.rows, 8), self.rows), slice(None)

    def eight(self, dy):
        first = self.at * SIDE * OWNED + dy * OWNED * self.rows
        return pl.ds(pl.multiple_of(first, 8), OWNED * self.rows), slice(None)

    def one(self, dy, j):
        first = self.at * SIDE * OWNED + (dy * OWNED + j) * self.rows
        return pl.ds(pl.multiple_of(first, 8), self.rows), slice(None)


def kernel(
    dest, trim, coef, rtap, ctap, img_hbm, wgt_hbm, res,
    img, wgt, kept, nums, rl, cc, xr, wsp, send, recv, acc, msend, mrecv,
    permv, perms, tabv, tabs, csend, crecv, ysend, yrecv,
    i_sem, w_sem, s_sem, r_sem, ms_sem, mr_sem, cs_sem, cr_sem, ys_sem, yr_sem, t_sem,
):
    visit, patch = lax.axis_index("visit"), lax.axis_index("patch")
    y, core = visit // 2, visit % 2
    z, x = patch // SIDE, patch % SIDE

    def column(d):
        dz, dx = SHIFTS[d]
        return lax.rem(z + dz, SIDE) * SIDE + lax.rem(x + dx, SIDE)

    def in_y(dy):
        return lax.rem(y + dy, SIDE) * 2 + core

    part_rows = WEIGHT_GROUPS[0][1]

    def load_weight(q):
        part = (slice(None), pl.ds(q * part_rows, part_rows), slice(None))
        return pltpu.make_async_copy(wgt_hbm.at[part], wgt.at[part], w_sem.at[q])

    for q in range(WEIGHT_CHUNKS):
        load_weight(q).start()
    load_image = pltpu.make_async_copy(img_hbm, img, i_sem)
    load_image.start()

    partners = [(visit, column(d)) for d in range(1, PLANE)]
    partners += [(visit + 1 - 2 * core, patch)]
    partners += [(in_y(dy), patch) for dy in range(1, SIDE)]
    barrier = pltpu.get_barrier_semaphore()
    for partner in partners:
        pl.semaphore_signal(barrier, inc=1, device_id=partner, device_id_type=MESH)

    row_of = lax.broadcasted_iota(I32, (TILE, TILE), 0)
    lane_of = lax.broadcasted_iota(I32, (TILE, TILE), 1)
    sub_of = lax.broadcasted_iota(I32, (8, TILE), 0)

    rows_c, lanes_c = row_of[:COUNT], lane_of[:COUNT]
    by_row = jnp.zeros((COUNT, TILE), I32)
    by_lane = jnp.full((COUNT, TILE), -1, I32)
    for n in range(COUNT):
        place = (dest[n] >> 3) & (PLANE - 1)
        by_row = jnp.where(rows_c == n, place, by_row)
        by_lane = jnp.where(lanes_c == n, place, by_lane)
    earlier = (by_row == by_lane) & (lanes_c < rows_c)
    rank = jnp.sum(earlier.astype(I32), axis=1, keepdims=True)
    tile_of = jnp.where(by_row * 8 + rank == lanes_c, rows_c, COUNT)
    permv[...] = jnp.broadcast_to(jnp.min(tile_of, axis=0, keepdims=True), (8, TILE))
    move = pltpu.make_async_copy(permv, perms, t_sem)
    move.start()

    rows_p, lanes_p = row_of[:part_rows], lane_of[:part_rows]

    def keep(chunk):
        load_weight(chunk.c).wait()
        rows_here = rows_p + chunk.start
        part = pl.ds(chunk.start, chunk.rows)

        def one(n, _):
            inside = (rows_here >= trim[0, n]) & (rows_here < TILE - trim[1, n])
            inside &= (lanes_p >= trim[2, n]) & (lanes_p < TILE - trim[3, n])
            kept[n, part, :] = jnp.where(inside, wgt[n, part, :], 0.0)
            return 0

        lax.fori_loop(0, COUNT, one, 0)

    keep(Chunk(0, 0, part_rows, 0))
    kept[COUNT] = jnp.zeros((TILE, TILE), F32)
    nums[COUNT] = jnp.zeros((TILE, TILE), F32)
    move.wait()

    def tile_in(d, k):
        return jnp.clip(perms[0, column(d) * 8 + k], 0, COUNT)

    def remote(src, dst, send_sem, recv_sem, to):
        return pltpu.make_async_remote_copy(
            src_ref=src, dst_ref=dst, send_sem=send_sem, recv_sem=recv_sem,
            device_id=to, device_id_type=MESH,
        )

    def meta_copy(d):
        return remote(msend.at[d], mrecv.at[d], ms_sem.at[d], mr_sem.at[d], (visit, column(d)))

    def plane_copy(chunk, d, to):
        part = chunk.slots(d)
        c = chunk.c
        return remote(send.at[part], recv.at[part], s_sem.at[c, d], r_sem.at[c, d], (visit, to))

    def core_copy(chunk, dy):
        part = chunk.eight(dy)
        to = (visit + 1 - 2 * core, patch)
        c = chunk.c
        return remote(csend.at[part], crecv.at[part], cs_sem.at[c, dy], cr_sem.at[c, dy], to)

    def y_copy(chunk, dy):
        part = chunk.eight(dy)
        c = chunk.c
        to = (in_y(dy), patch)
        return remote(ysend.at[part], yrecv.at[part], ys_sem.at[c, dy], yr_sem.at[c, dy], to)

    def fill(source, chunk, d):
        target = recv if d == 0 else send
        for k in range(SLOTS):
            block = source[tile_in(d, k), pl.ds(chunk.start, chunk.rows), :]
            target[chunk.slot(d, k)] = block

    def send_chunk(source, chunk):
        for d in range(1, PLANE):
            fill(source, chunk, d)
            plane_copy(chunk, d, column(d)).start()
        fill(source, chunk, 0)

    def loop(groups, c, base, first, body):
        for start, rows, count in groups:

            def one(q, _, start=start, rows=rows, c=c):
                body(Chunk(c + q, start + q * rows, rows, base))
                return 0

            begin = min(first, count)
            lax.fori_loop(begin, count, one, 0)
            first -= begin
            c += count

    weight_args = (WEIGHT_GROUPS, 0, 0)
    pixel_args = (PIXEL_GROUPS, WEIGHT_CHUNKS, TILE)

    pl.semaphore_wait(barrier, len(partners))
    send_chunk(kept, Chunk(0, 0, WEIGHT_GROUPS[0][1], 0))
    for d in range(PLANE):
        rows = jnp.full((8, TILE), -1, I32)
        for k in range(SLOTS):
            n = tile_in(d, k)
            to = dest[jnp.minimum(n, COUNT - 1)]
            row = jnp.where(n < COUNT, to // (OWNED * PLANE) * OWNED + to % OWNED, -1)
            rows = jnp.where(sub_of == k, row, rows)
        if d == 0:
            mrecv[0] = rows
        else:
            msend[d] = rows
            meta_copy(d).start()

    def weigh(chunk):
        keep(chunk)
        send_chunk(kept, chunk)

    loop(*weight_args, 1, weigh)

    half_row = lax.broadcasted_iota(I32, (TILE // 2, 2 * TILE), 0)
    half_lane = lax.broadcasted_iota(I32, (TILE // 2, 2 * TILE), 1)
    piece = (half_lane >= WINDOW).astype(I32) + (half_lane >= 2 * WINDOW).astype(I32)
    place = half_lane - piece * WINDOW

    def tables(k, _):
        for h in range(2):
            offset = place + h * (TILE - WINDOW) - half_row - h * (TILE // 2) + TAPS // 2
            offset = jnp.where(half_lane < 3 * WINDOW, offset, -1)
            taps = jnp.zeros((TILE // 2, 2 * TILE), F32)
            for index in range(TAPS):
                taps = jnp.where(offset == index, rtap[k, index], taps)
            high = taps.astype(BF16).astype(F32)
            rl[h, pl.ds(k * (TILE // 2), TILE // 2), :] = jnp.where(
                piece == 2, taps - high, high
            ).astype(BF16)
        offset = row_of - lane_of + TAPS // 2
        taps = jnp.zeros((TILE, TILE), F32)
        for index in range(TAPS):
            taps = jnp.where(offset == index, ctap[k, index], taps)
        high = taps.astype(BF16)
        cc[pl.ds(k * TILE, TILE), 0:TILE] = high
        cc[pl.ds(k * TILE, TILE), TILE:] = (taps - high.astype(F32)).astype(BF16)
        return 0

    lax.fori_loop(0, NB, tables, 0)
    load_image.wait()
    for h in range(2):
        xr[h, 3 * WINDOW:, :] = jnp.zeros((2 * TILE - 3 * WINDOW, 2 * TILE), BF16)

    def match(i, _):
        for pair in range(QUAD // 2):
            for u in range(2):
                pixels = img[i * QUAD + pair * 2 + u]
                high = pixels.astype(BF16)
                low = (pixels - high.astype(F32)).astype(BF16)
                lanes = slice(u * TILE, (u + 1) * TILE)
                for h in range(2):
                    a = h * (TILE - WINDOW)
                    xr[h, 0:WINDOW, lanes] = high[a:a + WINDOW]
                    xr[h, WINDOW:2 * WINDOW, lanes] = low[a:a + WINDOW]
                    xr[h, 2 * WINDOW:3 * WINDOW, lanes] = high[a:a + WINDOW]
            for h in range(2):
                for g in range(0, NB, 4):
                    down = jnp.dot(
                        rl[h, g * (TILE // 2):(g + 4) * (TILE // 2), :], xr[h],
                        preferred_element_type=F32,
                    )
                    for k in range(g, g + 4):
                        for u in range(2):
                            t = pair * 2 + u
                            b = (k - g) * (TILE // 2)
                            w = down[b:b + TILE // 2, u * TILE:(u + 1) * TILE]
                            w = w * coef[k, i * QUAD + t]
                            high = w.astype(BF16)
                            r = t * TILE + h * (TILE // 2)
                            lanes = slice(k * TILE, (k + 1) * TILE)
                            wsp[r:r + TILE // 2, lanes] = high
                            r += QUAD * TILE
                            wsp[r:r + TILE // 2, lanes] = (w - high.astype(F32)).astype(BF16)
        both = jnp.dot(wsp[...], cc[...], preferred_element_type=F32)
        both = both[:, :TILE] + both[:, TILE:]
        for t in range(QUAD):
            n = i * QUAD + t
            matched = both[t * TILE:(t + 1) * TILE]
            matched = matched + both[(QUAD + t) * TILE:(QUAD + t + 1) * TILE]
            nums[n] = kept[n] * matched
        return 0

    lax.fori_loop(0, COUNT // QUAD, match, 0)
    loop(*pixel_args, 0, lambda chunk: send_chunk(nums, chunk))

    for d in range(1, PLANE):
        meta_copy(d).wait()
    along = mrecv[...].reshape(TILE, TILE)
    across = along.T
    before = jnp.where((along == across) & (row_of < lane_of), row_of, -1)
    before = jnp.max(before, axis=0, keepdims=True)
    last = jnp.max(jnp.where(along == lane_of, row_of, -1), axis=0, keepdims=True)
    table = jnp.where(sub_of == 0, before, last)
    tabv[...] = jnp.where(table < 0, TILE, table)
    move = pltpu.make_async_copy(tabv, tabs, t_sem)
    move.start()
    move.wait()
    acc[TILE] = jnp.zeros((MOST, TILE), F32)

    def entry(r, s):
        return jnp.clip(tabs[r, s], 0, TILE)

    def gather(chunk):
        rows = chunk.rows

        def add(d):
            for k in range(SLOTS):
                s = d * 8 + k
                acc[s, :rows] = recv[chunk.slot(d, k)] + acc[entry(0, s), :rows]

        def one(d, _):
            plane_copy(chunk, d, column(1)).wait_recv()
            add(d)
            return 0

        add(0)
        lax.fori_loop(1, PLANE, one, 0)
        for dy in Y_ORDER:
            group = lax.rem(y + dy, SIDE) * 2
            for j in range(OWNED):
                csend[chunk.one(dy, j)] = acc[entry(1, (group + 1 - core) * OWNED + j), :rows]
            core_copy(chunk, dy).start()
        for dy in Y_ORDER:
            group = lax.rem(y + dy, SIDE) * 2
            for j in range(OWNED):
                ysend[chunk.one(dy, j)] = acc[entry(1, (group + core) * OWNED + j), :rows]

    def spread(chunk):
        for dy in Y_ORDER:
            part = chunk.eight(dy)
            core_copy(chunk, dy).wait_recv()
            ysend[part] = ysend[part] + crecv[part]
            if dy:
                y_copy(chunk, dy).start()

    def drain(chunk):
        def one(d, _):
            plane_copy(chunk, d, column(1)).wait_send()
            return 0

        lax.fori_loop(1, PLANE, one, 0)
        for dy in range(SIDE):
            core_copy(chunk, dy).wait_send()
            if dy:
                y_copy(chunk, dy).wait_send()

    def total(chunk):
        for dy in range(1, SIDE):
            y_copy(chunk, dy).wait_recv()
        a, b, c, d = (chunk.eight(dy) for dy in range(SIDE))
        return (ysend[a] + yrecv[b]) + (yrecv[c] + yrecv[d])

    def weights(chunk):
        gather(chunk)
        spread(chunk)

    def sums(chunk):
        value = total(chunk) + 1.0
        for j in range(OWNED):
            block = value[j * chunk.rows:(j + 1) * chunk.rows]
            res[j, pl.ds(chunk.start, chunk.rows), :] = block

    def finish(chunk):
        value = total(chunk)
        for j in range(OWNED):
            part = (j, pl.ds(chunk.start, chunk.rows), slice(None))
            res[part] = value[j * chunk.rows:(j + 1) * chunk.rows] / res[part]

    loop(*weight_args, 0, weights)
    loop(*weight_args, 0, sums)
    loop(*weight_args, 0, drain)

    pixel_chunks = []
    c = WEIGHT_CHUNKS
    for start, rows, count in PIXEL_GROUPS:
        for q in range(count):
            pixel_chunks.append(Chunk(c, start + q * rows, rows, TILE))
            c += 1
    for index, chunk in enumerate(pixel_chunks):
        gather(chunk)
        spread(chunk)
        if index:
            finish(pixel_chunks[index - 1])
        if index > 1:
            drain(pixel_chunks[index - 2])
    finish(pixel_chunks[-1])
    for chunk in pixel_chunks[-2:]:
        drain(chunk)


def shards(image, weight, coeffs, trim, destination, row_taps, col_taps):
    smem = pl.BlockSpec(memory_space=pltpu.SMEM)
    hbm = pl.BlockSpec(memory_space=pl.ANY)
    dma = pltpu.SemaphoreType.DMA
    stack = 2 * TILE * SIDE * OWNED
    return pl.pallas_call(
        kernel,
        out_shape=pltpu.VMEM((OWNED, TILE, TILE), F32),
        in_specs=[smem] * 5 + [hbm] * 2,
        out_specs=pl.BlockSpec(memory_space=pltpu.VMEM),
        scratch_shapes=[
            pltpu.VMEM((COUNT, TILE, TILE), F32),
            pltpu.VMEM((COUNT, TILE, TILE), F32),
            pltpu.VMEM((COUNT + 1, TILE, TILE), F32),
            pltpu.VMEM((COUNT + 1, TILE, TILE), F32),
            pltpu.VMEM((2, NB * TILE // 2, 2 * TILE), BF16),
            pltpu.VMEM((NB * TILE, 2 * TILE), BF16),
            pltpu.VMEM((2, 2 * TILE, 2 * TILE), BF16),
            pltpu.VMEM((2 * QUAD * TILE, NB * TILE), BF16),
            pltpu.VMEM((PLANE, 2 * TILE * SLOTS, TILE), F32),
            pltpu.VMEM((PLANE, 2 * TILE * SLOTS, TILE), F32),
            pltpu.VMEM((TILE + 1, MOST, TILE), F32),
            pltpu.VMEM((PLANE, 8, TILE), I32),
            pltpu.VMEM((PLANE, 8, TILE), I32),
            pltpu.VMEM((8, TILE), I32),
            pltpu.SMEM((8, TILE), I32),
            pltpu.VMEM((8, TILE), I32),
            pltpu.SMEM((8, TILE), I32),
            pltpu.VMEM((stack, TILE), F32),
            pltpu.VMEM((stack, TILE), F32),
            pltpu.VMEM((stack, TILE), F32),
            pltpu.VMEM((stack, TILE), F32),
            dma(()),
            dma((WEIGHT_CHUNKS,)),
            dma((CHUNKS, PLANE)),
            dma((CHUNKS, PLANE)),
            dma((PLANE,)),
            dma((PLANE,)),
            dma((CHUNKS, SIDE)),
            dma((CHUNKS, SIDE)),
            dma((CHUNKS, SIDE)),
            dma((CHUNKS, SIDE)),
            dma(()),
        ],
        compiler_params=pltpu.CompilerParams(
            collective_id=0, has_side_effects=True, vmem_limit_bytes=60 << 20
        ),
        name="coadd",
    )(destination, trim.T, coeffs.T, row_taps, col_taps, image, weight)


def solution(mesh):
    placed = (
        P(("visit", "patch"), None, None),
        P(("visit", "patch"), None, None),
        P(("visit", "patch"), None),
        P(("visit", "patch"), None),
        P(("visit", "patch")),
        P(),
        P(),
    )
    return jax.shard_map(
        shards,
        mesh=mesh,
        in_specs=placed,
        out_specs=P(("visit", "patch"), None, None),
        check_vma=False,
    )
```

```python
import jax
import jax.numpy as jnp
from jax import lax
from jax.experimental import pallas as pl
from jax.experimental.pallas import tpu as pltpu
from jax.sharding import PartitionSpec as P

MESH = pl.DeviceIdType.MESH
F32 = jnp.float32
BF16 = jnp.bfloat16
I32 = jnp.int32

TILE = 128
TAPS = 21
NB = 16
COUNT = 32
OWNED = 8
SLOTS = 5
WINDOW = 80
QUAD = 4

WEIGHT_GROUPS = ((0, 32, 4),)
PIXEL_GROUPS = ((0, 40, 2), (80, 24, 1), (104, 16, 1), (120, 8, 1))
WEIGHT_CHUNKS = sum(g[2] for g in WEIGHT_GROUPS)
CHUNKS = WEIGHT_CHUNKS + sum(g[2] for g in PIXEL_GROUPS)
MOST = 40

SHIFTS = (
    (0, 0),
    (2, 2),
    (1, 2), (2, 1), (3, 2), (2, 3),
    (2, 0), (0, 2),
    (1, 1), (3, 3),
    (1, 3), (3, 1),
    (0, 1), (1, 0), (0, 3), (3, 0),
)
SIDE = 4
PLANE = len(SHIFTS)
Y_ORDER = (2, 1, 3, 0)


class Chunk:
    def __init__(self, c, start, rows, base):
        self.c, self.start, self.rows = c, start, rows
        self.at = base + start

    def slots(self, d):
        return d, pl.ds(pl.multiple_of(self.at * SLOTS, 8), self.rows * SLOTS), slice(None)

    def slot(self, d, k):
        return d, pl.ds(pl.multiple_of(self.at * SLOTS + k * self.rows, 8), self.rows), slice(None)

    def eight(self, dy):
        first = self.at * SIDE * OWNED + dy * OWNED * self.rows
        return pl.ds(pl.multiple_of(first, 8), OWNED * self.rows), slice(None)

    def one(self, dy, j):
        first = self.at * SIDE * OWNED + (dy * OWNED + j) * self.rows
        return pl.ds(pl.multiple_of(first, 8), self.rows), slice(None)


def kernel(
    dest, trim, coef, rtap, ctap, img_hbm, wgt_hbm, res,
    img, wgt, kept, nums, rl, cc, xr, wsp, send, recv, acc, msend, mrecv,
    permv, perms, tabv, tabs, csend, crecv, ysend, yrecv,
    i_sem, w_sem, s_sem, r_sem, ms_sem, mr_sem, cs_sem, cr_sem, ys_sem, yr_sem, t_sem,
):
    visit, patch = lax.axis_index("visit"), lax.axis_index("patch")
    y, core = visit // 2, visit % 2
    z, x = patch // SIDE, patch % SIDE

    def column(d):
        dz, dx = SHIFTS[d]
        return lax.rem(z + dz, SIDE) * SIDE + lax.rem(x + dx, SIDE)

    def in_y(dy):
        return lax.rem(y + dy, SIDE) * 2 + core

    part_rows = WEIGHT_GROUPS[0][1]

    def load_weight(q):
        part = (slice(None), pl.ds(q * part_rows, part_rows), slice(None))
        return pltpu.make_async_copy(wgt_hbm.at[part], wgt.at[part], w_sem.at[q])

    for q in range(WEIGHT_CHUNKS):
        load_weight(q).start()
    load_image = pltpu.make_async_copy(img_hbm, img, i_sem)
    load_image.start()

    partners = [(visit, column(d)) for d in range(1, PLANE)]
    partners += [(visit + 1 - 2 * core, patch)]
    partners += [(in_y(dy), patch) for dy in range(1, SIDE)]
    barrier = pltpu.get_barrier_semaphore()
    for partner in partners:
        pl.semaphore_signal(barrier, inc=1, device_id=partner, device_id_type=MESH)

    row_of = lax.broadcasted_iota(I32, (TILE, TILE), 0)
    lane_of = lax.broadcasted_iota(I32, (TILE, TILE), 1)
    sub_of = lax.broadcasted_iota(I32, (8, TILE), 0)

    rows_c, lanes_c = row_of[:COUNT], lane_of[:COUNT]
    by_row = jnp.zeros((COUNT, TILE), I32)
    by_lane = jnp.full((COUNT, TILE), -1, I32)
    for n in range(COUNT):
        place = (dest[n] >> 3) & (PLANE - 1)
        by_row = jnp.where(rows_c == n, place, by_row)
        by_lane = jnp.where(lanes_c == n, place, by_lane)
    earlier = (by_row == by_lane) & (lanes_c < rows_c)
    rank = jnp.sum(earlier.astype(I32), axis=1, keepdims=True)
    tile_of = jnp.where(by_row * 8 + rank == lanes_c, rows_c, COUNT)
    permv[...] = jnp.broadcast_to(jnp.min(tile_of, axis=0, keepdims=True), (8, TILE))
    move = pltpu.make_async_copy(permv, perms, t_sem)
    move.start()

    rows_p, lanes_p = row_of[:part_rows], lane_of[:part_rows]

    def keep(chunk):
        load_weight(chunk.c).wait()
        rows_here = rows_p + chunk.start
        part = pl.ds(chunk.start, chunk.rows)

        def one(n, _):
            inside = (rows_here >= trim[0, n]) & (rows_here < TILE - trim[1, n])
            inside &= (lanes_p >= trim[2, n]) & (lanes_p < TILE - trim[3, n])
            kept[n, part, :] = jnp.where(inside, wgt[n, part, :], 0.0)
            return 0

        lax.fori_loop(0, COUNT, one, 0)

    keep(Chunk(0, 0, part_rows, 0))
    kept[COUNT] = jnp.zeros((TILE, TILE), F32)
    nums[COUNT] = jnp.zeros((TILE, TILE), F32)
    move.wait()

    def tile_in(d, k):
        return jnp.clip(perms[0, column(d) * 8 + k], 0, COUNT)

    def remote(src, dst, send_sem, recv_sem, to):
        return pltpu.make_async_remote_copy(
            src_ref=src, dst_ref=dst, send_sem=send_sem, recv_sem=recv_sem,
            device_id=to, device_id_type=MESH,
        )

    def meta_copy(d):
        return remote(msend.at[d], mrecv.at[d], ms_sem.at[d], mr_sem.at[d], (visit, column(d)))

    def plane_copy(chunk, d, to):
        part = chunk.slots(d)
        c = chunk.c
        return remote(send.at[part], recv.at[part], s_sem.at[c, d], r_sem.at[c, d], (visit, to))

    def core_copy(chunk, dy):
        part = chunk.eight(dy)
        to = (visit + 1 - 2 * core, patch)
        c = chunk.c
        return remote(csend.at[part], crecv.at[part], cs_sem.at[c, dy], cr_sem.at[c, dy], to)

    def y_copy(chunk, dy):
        part = chunk.eight(dy)
        c = chunk.c
        to = (in_y(dy), patch)
        return remote(ysend.at[part], yrecv.at[part], ys_sem.at[c, dy], yr_sem.at[c, dy], to)

    def fill(source, chunk, d):
        target = recv if d == 0 else send
        for k in range(SLOTS):
            block = source[tile_in(d, k), pl.ds(chunk.start, chunk.rows), :]
            target[chunk.slot(d, k)] = block

    def send_chunk(source, chunk):
        for d in range(1, PLANE):
            fill(source, chunk, d)
            plane_copy(chunk, d, column(d)).start()
        fill(source, chunk, 0)

    def loop(groups, c, base, first, body):
        for start, rows, count in groups:

            def one(q, _, start=start, rows=rows, c=c):
                body(Chunk(c + q, start + q * rows, rows, base))
                return 0

            begin = min(first, count)
            lax.fori_loop(begin, count, one, 0)
            first -= begin
            c += count

    weight_args = (WEIGHT_GROUPS, 0, 0)
    pixel_args = (PIXEL_GROUPS, WEIGHT_CHUNKS, TILE)

    pl.semaphore_wait(barrier, len(partners))
    send_chunk(kept, Chunk(0, 0, WEIGHT_GROUPS[0][1], 0))
    for d in range(PLANE):
        rows = jnp.full((8, TILE), -1, I32)
        for k in range(SLOTS):
            n = tile_in(d, k)
            to = dest[jnp.minimum(n, COUNT - 1)]
            row = jnp.where(n < COUNT, to // (OWNED * PLANE) * OWNED + to % OWNED, -1)
            rows = jnp.where(sub_of == k, row, rows)
        if d == 0:
            mrecv[0] = rows
        else:
            msend[d] = rows
            meta_copy(d).start()

    def weigh(chunk):
        keep(chunk)
        send_chunk(kept, chunk)

    loop(*weight_args, 1, weigh)

    half_row = lax.broadcasted_iota(I32, (TILE // 2, 2 * TILE), 0)
    half_lane = lax.broadcasted_iota(I32, (TILE // 2, 2 * TILE), 1)
    piece = (half_lane >= WINDOW).astype(I32) + (half_lane >= 2 * WINDOW).astype(I32)
    place = half_lane - piece * WINDOW

    def tables(k, _):
        for h in range(2):
            offset = place + h * (TILE - WINDOW) - half_row - h * (TILE // 2) + TAPS // 2
            offset = jnp.where(half_lane < 3 * WINDOW, offset, -1)
            taps = jnp.zeros((TILE // 2, 2 * TILE), F32)
            for index in range(TAPS):
                taps = jnp.where(offset == index, rtap[k, index], taps)
            high = taps.astype(BF16).astype(F32)
            rl[h, pl.ds(k * (TILE // 2), TILE // 2), :] = jnp.where(
                piece == 2, taps - high, high
            ).astype(BF16)
        offset = row_of - lane_of + TAPS // 2
        taps = jnp.zeros((TILE, TILE), F32)
        for index in range(TAPS):
            taps = jnp.where(offset == index, ctap[k, index], taps)
        high = taps.astype(BF16)
        cc[pl.ds(k * TILE, TILE), 0:TILE] = high
        cc[pl.ds(k * TILE, TILE), TILE:] = (taps - high.astype(F32)).astype(BF16)
        return 0

    lax.fori_loop(0, NB, tables, 0)
    load_image.wait()
    for h in range(2):
        xr[h, 3 * WINDOW:, :] = jnp.zeros((2 * TILE - 3 * WINDOW, 2 * TILE), BF16)

    def match(i, _):
        for pair in range(QUAD // 2):
            for u in range(2):
                pixels = img[i * QUAD + pair * 2 + u]
                high = pixels.astype(BF16)
                low = (pixels - high.astype(F32)).astype(BF16)
                lanes = slice(u * TILE, (u + 1) * TILE)
                for h in range(2):
                    a = h * (TILE - WINDOW)
                    xr[h, 0:WINDOW, lanes] = high[a:a + WINDOW]
                    xr[h, WINDOW:2 * WINDOW, lanes] = low[a:a + WINDOW]
                    xr[h, 2 * WINDOW:3 * WINDOW, lanes] = high[a:a + WINDOW]
            for h in range(2):
                for g in range(0, NB, 4):
                    down = jnp.dot(
                        rl[h, g * (TILE // 2):(g + 4) * (TILE // 2), :], xr[h],
                        preferred_element_type=F32,
                    )
                    for k in range(g, g + 4):
                        for u in range(2):
                            t = pair * 2 + u
                            b = (k - g) * (TILE // 2)
                            w = down[b:b + TILE // 2, u * TILE:(u + 1) * TILE]
                            w = w * coef[k, i * QUAD + t]
                            high = w.astype(BF16)
                            r = t * TILE + h * (TILE // 2)
                            lanes = slice(k * TILE, (k + 1) * TILE)
                            wsp[r:r + TILE // 2, lanes] = high
                            r += QUAD * TILE
                            wsp[r:r + TILE // 2, lanes] = (w - high.astype(F32)).astype(BF16)
        both = jnp.dot(wsp[...], cc[...], preferred_element_type=F32)
        both = both[:, :TILE] + both[:, TILE:]
        for t in range(QUAD):
            n = i * QUAD + t
            matched = both[t * TILE:(t + 1) * TILE]
            matched = matched + both[(QUAD + t) * TILE:(QUAD + t + 1) * TILE]
            nums[n] = kept[n] * matched
        return 0

    lax.fori_loop(0, COUNT // QUAD, match, 0)
    loop(*pixel_args, 0, lambda chunk: send_chunk(nums, chunk))

    for d in range(1, PLANE):
        meta_copy(d).wait()
    along = mrecv[...].reshape(TILE, TILE)
    across = along.T
    before = jnp.where((along == across) & (row_of < lane_of), row_of, -1)
    before = jnp.max(before, axis=0, keepdims=True)
    last = jnp.max(jnp.where(along == lane_of, row_of, -1), axis=0, keepdims=True)
    table = jnp.where(sub_of == 0, before, last)
    tabv[...] = jnp.where(table < 0, TILE, table)
    move = pltpu.make_async_copy(tabv, tabs, t_sem)
    move.start()
    move.wait()
    acc[TILE] = jnp.zeros((MOST, TILE), F32)

    def entry(r, s):
        return jnp.clip(tabs[r, s], 0, TILE)

    def gather(chunk):
        rows = chunk.rows

        def add(d):
            for k in range(SLOTS):
                s = d * 8 + k
                acc[s, :rows] = recv[chunk.slot(d, k)] + acc[entry(0, s), :rows]

        def one(d, _):
            plane_copy(chunk, d, column(1)).wait_recv()
            add(d)
            return 0

        add(0)
        lax.fori_loop(1, PLANE, one, 0)
        for dy in Y_ORDER:
            group = lax.rem(y + dy, SIDE) * 2
            for j in range(OWNED):
                csend[chunk.one(dy, j)] = acc[entry(1, (group + 1 - core) * OWNED + j), :rows]
            core_copy(chunk, dy).start()
        for dy in Y_ORDER:
            group = lax.rem(y + dy, SIDE) * 2
            for j in range(OWNED):
                ysend[chunk.one(dy, j)] = acc[entry(1, (group + core) * OWNED + j), :rows]

    def spread(chunk):
        for dy in Y_ORDER:
            part = chunk.eight(dy)
            core_copy(chunk, dy).wait_recv()
            ysend[part] = ysend[part] + crecv[part]
            if dy:
                y_copy(chunk, dy).start()

    def drain(chunk):
        def one(d, _):
            plane_copy(chunk, d, column(1)).wait_send()
            return 0

        lax.fori_loop(1, PLANE, one, 0)
        for dy in range(SIDE):
            core_copy(chunk, dy).wait_send()
            if dy:
                y_copy(chunk, dy).wait_send()

    def total(chunk):
        for dy in range(1, SIDE):
            y_copy(chunk, dy).wait_recv()
        a, b, c, d = (chunk.eight(dy) for dy in range(SIDE))
        return (ysend[a] + yrecv[b]) + (yrecv[c] + yrecv[d])

    def weights(chunk):
        gather(chunk)
        spread(chunk)

    def sums(chunk):
        value = total(chunk) + 1.0
        for j in range(OWNED):
            block = value[j * chunk.rows:(j + 1) * chunk.rows]
            res[j, pl.ds(chunk.start, chunk.rows), :] = block

    def finish(chunk):
        value = total(chunk)
        for j in range(OWNED):
            part = (j, pl.ds(chunk.start, chunk.rows), slice(None))
            res[part] = value[j * chunk.rows:(j + 1) * chunk.rows] / res[part]

    loop(*weight_args, 0, weights)
    loop(*weight_args, 0, sums)
    loop(*weight_args, 0, drain)

    pixel_chunks = []
    c = WEIGHT_CHUNKS
    for start, rows, count in PIXEL_GROUPS:
        for q in range(count):
            pixel_chunks.append(Chunk(c, start + q * rows, rows, TILE))
            c += 1
    undrained = []
    for index, chunk in enumerate(pixel_chunks):
        gather(chunk)
        spread(chunk)
        if index:
            finish(pixel_chunks[index - 1])
        if index + 1 == len(pixel_chunks):
            break
        undrained.append(chunk)
        if index > 1 and index + 2 < len(pixel_chunks):
            drain(undrained.pop(0))
    finish(pixel_chunks[-1])
    for chunk in undrained + pixel_chunks[-1:]:
        drain(chunk)


def shards(image, weight, coeffs, trim, destination, row_taps, col_taps):
    smem = pl.BlockSpec(memory_space=pltpu.SMEM)
    hbm = pl.BlockSpec(memory_space=pl.ANY)
    dma = pltpu.SemaphoreType.DMA
    stack = 2 * TILE * SIDE * OWNED
    return pl.pallas_call(
        kernel,
        out_shape=pltpu.VMEM((OWNED, TILE, TILE), F32),
        in_specs=[smem] * 5 + [hbm] * 2,
        out_specs=pl.BlockSpec(memory_space=pltpu.VMEM),
        scratch_shapes=[
            pltpu.VMEM((COUNT, TILE, TILE), F32),
            pltpu.VMEM((COUNT, TILE, TILE), F32),
            pltpu.VMEM((COUNT + 1, TILE, TILE), F32),
            pltpu.VMEM((COUNT + 1, TILE, TILE), F32),
            pltpu.VMEM((2, NB * TILE // 2, 2 * TILE), BF16),
            pltpu.VMEM((NB * TILE, 2 * TILE), BF16),
            pltpu.VMEM((2, 2 * TILE, 2 * TILE), BF16),
            pltpu.VMEM((2 * QUAD * TILE, NB * TILE), BF16),
            pltpu.VMEM((PLANE, 2 * TILE * SLOTS, TILE), F32),
            pltpu.VMEM((PLANE, 2 * TILE * SLOTS, TILE), F32),
            pltpu.VMEM((TILE + 1, MOST, TILE), F32),
            pltpu.VMEM((PLANE, 8, TILE), I32),
            pltpu.VMEM((PLANE, 8, TILE), I32),
            pltpu.VMEM((8, TILE), I32),
            pltpu.SMEM((8, TILE), I32),
            pltpu.VMEM((8, TILE), I32),
            pltpu.SMEM((8, TILE), I32),
            pltpu.VMEM((stack, TILE), F32),
            pltpu.VMEM((stack, TILE), F32),
            pltpu.VMEM((stack, TILE), F32),
            pltpu.VMEM((stack, TILE), F32),
            dma(()),
            dma((WEIGHT_CHUNKS,)),
            dma((CHUNKS, PLANE)),
            dma((CHUNKS, PLANE)),
            dma((PLANE,)),
            dma((PLANE,)),
            dma((CHUNKS, SIDE)),
            dma((CHUNKS, SIDE)),
            dma((CHUNKS, SIDE)),
            dma((CHUNKS, SIDE)),
            dma(()),
        ],
        compiler_params=pltpu.CompilerParams(
            collective_id=0, has_side_effects=True, vmem_limit_bytes=60 << 20
        ),
        name="coadd",
    )(destination, trim.T, coeffs.T, row_taps, col_taps, image, weight)


def solution(mesh):
    placed = (
        P(("visit", "patch"), None, None),
        P(("visit", "patch"), None, None),
        P(("visit", "patch"), None),
        P(("visit", "patch"), None),
        P(("visit", "patch")),
        P(),
        P(),
    )
    return jax.shard_map(
        shards,
        mesh=mesh,
        in_specs=placed,
        out_specs=P(("visit", "patch"), None, None),
        check_vma=False,
    )
```

```python
import jax
import jax.numpy as jnp
from jax import lax
from jax.experimental import pallas as pl
from jax.experimental.pallas import tpu as pltpu
from jax.sharding import PartitionSpec as P

MESH = pl.DeviceIdType.MESH
F32 = jnp.float32
BF16 = jnp.bfloat16
I32 = jnp.int32

TILE = 128
TAPS = 21
NB = 16
COUNT = 32
OWNED = 8
SLOTS = 5
WINDOW = 80
QUAD = 4

WEIGHT_GROUPS = ((0, 32, 4),)
PIXEL_GROUPS = ((0, 40, 2), (80, 24, 1), (104, 16, 1), (120, 8, 1))
WEIGHT_CHUNKS = sum(g[2] for g in WEIGHT_GROUPS)
CHUNKS = WEIGHT_CHUNKS + sum(g[2] for g in PIXEL_GROUPS)
MOST = 40

SHIFTS = (
    (0, 0),
    (2, 2),
    (3, 2), (2, 3), (1, 2), (2, 1),
    (2, 0), (0, 2),
    (1, 3), (3, 1),
    (1, 1), (3, 3),
    (0, 3), (3, 0), (0, 1), (1, 0),
)
SIDE = 4
PLANE = len(SHIFTS)
Y_ORDER = (2, 1, 3, 0)


class Chunk:
    def __init__(self, c, start, rows, base):
        self.c, self.start, self.rows = c, start, rows
        self.at = base + start

    def slots(self, d):
        return d, pl.ds(pl.multiple_of(self.at * SLOTS, 8), self.rows * SLOTS), slice(None)

    def slot(self, d, k):
        return d, pl.ds(pl.multiple_of(self.at * SLOTS + k * self.rows, 8), self.rows), slice(None)

    def eight(self, dy):
        first = self.at * SIDE * OWNED + dy * OWNED * self.rows
        return pl.ds(pl.multiple_of(first, 8), OWNED * self.rows), slice(None)

    def one(self, dy, j):
        first = self.at * SIDE * OWNED + (dy * OWNED + j) * self.rows
        return pl.ds(pl.multiple_of(first, 8), self.rows), slice(None)


def kernel(
    dest, trim, coef, rtap, ctap, img_hbm, wgt_hbm, res,
    img, wgt, kept, nums, rl, cc, xr, wsp, send, recv, acc, msend, mrecv,
    permv, perms, tabv, tabs, csend, crecv, ysend, yrecv,
    i_sem, w_sem, s_sem, r_sem, ms_sem, mr_sem, cs_sem, cr_sem, ys_sem, yr_sem, t_sem,
):
    visit, patch = lax.axis_index("visit"), lax.axis_index("patch")
    y, core = visit // 2, visit % 2
    z, x = patch // SIDE, patch % SIDE

    def column(d):
        dz, dx = SHIFTS[d]
        return lax.rem(z + dz, SIDE) * SIDE + lax.rem(x + dx, SIDE)

    def in_y(dy):
        return lax.rem(y + dy, SIDE) * 2 + core

    part_rows = WEIGHT_GROUPS[0][1]

    def load_weight(q):
        part = (slice(None), pl.ds(q * part_rows, part_rows), slice(None))
        return pltpu.make_async_copy(wgt_hbm.at[part], wgt.at[part], w_sem.at[q])

    for q in range(WEIGHT_CHUNKS):
        load_weight(q).start()
    load_image = pltpu.make_async_copy(img_hbm, img, i_sem)
    load_image.start()

    partners = [(visit, column(d)) for d in range(1, PLANE)]
    partners += [(visit + 1 - 2 * core, patch)]
    partners += [(in_y(dy), patch) for dy in range(1, SIDE)]
    barrier = pltpu.get_barrier_semaphore()
    for partner in partners:
        pl.semaphore_signal(barrier, inc=1, device_id=partner, device_id_type=MESH)

    row_of = lax.broadcasted_iota(I32, (TILE, TILE), 0)
    lane_of = lax.broadcasted_iota(I32, (TILE, TILE), 1)
    sub_of = lax.broadcasted_iota(I32, (8, TILE), 0)

    rows_c, lanes_c = row_of[:COUNT], lane_of[:COUNT]
    by_row = jnp.zeros((COUNT, TILE), I32)
    by_lane = jnp.full((COUNT, TILE), -1, I32)
    for n in range(COUNT):
        place = (dest[n] >> 3) & (PLANE - 1)
        by_row = jnp.where(rows_c == n, place, by_row)
        by_lane = jnp.where(lanes_c == n, place, by_lane)
    earlier = (by_row == by_lane) & (lanes_c < rows_c)
    rank = jnp.sum(earlier.astype(I32), axis=1, keepdims=True)
    tile_of = jnp.where(by_row * 8 + rank == lanes_c, rows_c, COUNT)
    permv[...] = jnp.broadcast_to(jnp.min(tile_of, axis=0, keepdims=True), (8, TILE))
    move = pltpu.make_async_copy(permv, perms, t_sem)
    move.start()

    rows_p, lanes_p = row_of[:part_rows], lane_of[:part_rows]

    def keep(chunk):
        load_weight(chunk.c).wait()
        rows_here = rows_p + chunk.start
        part = pl.ds(chunk.start, chunk.rows)

        def one(n, _):
            inside = (rows_here >= trim[0, n]) & (rows_here < TILE - trim[1, n])
            inside &= (lanes_p >= trim[2, n]) & (lanes_p < TILE - trim[3, n])
            kept[n, part, :] = jnp.where(inside, wgt[n, part, :], 0.0)
            return 0

        lax.fori_loop(0, COUNT, one, 0)

    keep(Chunk(0, 0, part_rows, 0))
    kept[COUNT] = jnp.zeros((TILE, TILE), F32)
    nums[COUNT] = jnp.zeros((TILE, TILE), F32)
    move.wait()

    def tile_in(d, k):
        return jnp.clip(perms[0, column(d) * 8 + k], 0, COUNT)

    def remote(src, dst, send_sem, recv_sem, to):
        return pltpu.make_async_remote_copy(
            src_ref=src, dst_ref=dst, send_sem=send_sem, recv_sem=recv_sem,
            device_id=to, device_id_type=MESH,
        )

    def meta_copy(d):
        return remote(msend.at[d], mrecv.at[d], ms_sem.at[d], mr_sem.at[d], (visit, column(d)))

    def plane_copy(chunk, d, to):
        part = chunk.slots(d)
        c = chunk.c
        return remote(send.at[part], recv.at[part], s_sem.at[c, d], r_sem.at[c, d], (visit, to))

    def core_copy(chunk, dy):
        part = chunk.eight(dy)
        to = (visit + 1 - 2 * core, patch)
        c = chunk.c
        return remote(csend.at[part], crecv.at[part], cs_sem.at[c, dy], cr_sem.at[c, dy], to)

    def y_copy(chunk, dy):
        part = chunk.eight(dy)
        c = chunk.c
        to = (in_y(dy), patch)
        return remote(ysend.at[part], yrecv.at[part], ys_sem.at[c, dy], yr_sem.at[c, dy], to)

    def fill(source, chunk, d):
        target = recv if d == 0 else send
        for k in range(SLOTS):
            block = source[tile_in(d, k), pl.ds(chunk.start, chunk.rows), :]
            target[chunk.slot(d, k)] = block

    def send_chunk(source, chunk):
        for d in range(1, PLANE):
            fill(source, chunk, d)
            plane_copy(chunk, d, column(d)).start()
        fill(source, chunk, 0)

    def loop(groups, c, base, first, body):
        for start, rows, count in groups:

            def one(q, _, start=start, rows=rows, c=c):
                body(Chunk(c + q, start + q * rows, rows, base))
                return 0

            begin = min(first, count)
            lax.fori_loop(begin, count, one, 0)
            first -= begin
            c += count

    weight_args = (WEIGHT_GROUPS, 0, 0)
    pixel_args = (PIXEL_GROUPS, WEIGHT_CHUNKS, TILE)

    pl.semaphore_wait(barrier, len(partners))
    send_chunk(kept, Chunk(0, 0, WEIGHT_GROUPS[0][1], 0))
    for d in range(PLANE):
        rows = jnp.full((8, TILE), -1, I32)
        for k in range(SLOTS):
            n = tile_in(d, k)
            to = dest[jnp.minimum(n, COUNT - 1)]
            row = jnp.where(n < COUNT, to // (OWNED * PLANE) * OWNED + to % OWNED, -1)
            rows = jnp.where(sub_of == k, row, rows)
        if d == 0:
            mrecv[0] = rows
        else:
            msend[d] = rows
            meta_copy(d).start()

    def weigh(chunk):
        keep(chunk)
        send_chunk(kept, chunk)

    loop(*weight_args, 1, weigh)

    half_row = lax.broadcasted_iota(I32, (TILE // 2, 2 * TILE), 0)
    half_lane = lax.broadcasted_iota(I32, (TILE // 2, 2 * TILE), 1)
    piece = (half_lane >= WINDOW).astype(I32) + (half_lane >= 2 * WINDOW).astype(I32)
    place = half_lane - piece * WINDOW

    def tables(k, _):
        for h in range(2):
            offset = place + h * (TILE - WINDOW) - half_row - h * (TILE // 2) + TAPS // 2
            offset = jnp.where(half_lane < 3 * WINDOW, offset, -1)
            taps = jnp.zeros((TILE // 2, 2 * TILE), F32)
            for index in range(TAPS):
                taps = jnp.where(offset == index, rtap[k, index], taps)
            high = taps.astype(BF16).astype(F32)
            rl[h, pl.ds(k * (TILE // 2), TILE // 2), :] = jnp.where(
                piece == 2, taps - high, high
            ).astype(BF16)
        offset = row_of - lane_of + TAPS // 2
        taps = jnp.zeros((TILE, TILE), F32)
        for index in range(TAPS):
            taps = jnp.where(offset == index, ctap[k, index], taps)
        high = taps.astype(BF16)
        cc[pl.ds(k * TILE, TILE), 0:TILE] = high
        cc[pl.ds(k * TILE, TILE), TILE:] = (taps - high.astype(F32)).astype(BF16)
        return 0

    lax.fori_loop(0, NB, tables, 0)
    load_image.wait()
    for h in range(2):
        xr[h, 3 * WINDOW:, :] = jnp.zeros((2 * TILE - 3 * WINDOW, 2 * TILE), BF16)

    def match(i, _):
        for pair in range(QUAD // 2):
            for u in range(2):
                pixels = img[i * QUAD + pair * 2 + u]
                high = pixels.astype(BF16)
                low = (pixels - high.astype(F32)).astype(BF16)
                lanes = slice(u * TILE, (u + 1) * TILE)
                for h in range(2):
                    a = h * (TILE - WINDOW)
                    xr[h, 0:WINDOW, lanes] = high[a:a + WINDOW]
                    xr[h, WINDOW:2 * WINDOW, lanes] = low[a:a + WINDOW]
                    xr[h, 2 * WINDOW:3 * WINDOW, lanes] = high[a:a + WINDOW]
            for h in range(2):
                for g in range(0, NB, 4):
                    down = jnp.dot(
                        rl[h, g * (TILE // 2):(g + 4) * (TILE // 2), :], xr[h],
                        preferred_element_type=F32,
                    )
                    for k in range(g, g + 4):
                        for u in range(2):
                            t = pair * 2 + u
                            b = (k - g) * (TILE // 2)
                            w = down[b:b + TILE // 2, u * TILE:(u + 1) * TILE]
                            w = w * coef[k, i * QUAD + t]
                            high = w.astype(BF16)
                            r = t * TILE + h * (TILE // 2)
                            lanes = slice(k * TILE, (k + 1) * TILE)
                            wsp[r:r + TILE // 2, lanes] = high
                            r += QUAD * TILE
                            wsp[r:r + TILE // 2, lanes] = (w - high.astype(F32)).astype(BF16)
        both = jnp.dot(wsp[...], cc[...], preferred_element_type=F32)
        both = both[:, :TILE] + both[:, TILE:]
        for t in range(QUAD):
            n = i * QUAD + t
            matched = both[t * TILE:(t + 1) * TILE]
            matched = matched + both[(QUAD + t) * TILE:(QUAD + t + 1) * TILE]
            nums[n] = kept[n] * matched
        return 0

    lax.fori_loop(0, COUNT // QUAD, match, 0)
    loop(*pixel_args, 0, lambda chunk: send_chunk(nums, chunk))

    for d in range(1, PLANE):
        meta_copy(d).wait()
    along = mrecv[...].reshape(TILE, TILE)
    across = along.T
    before = jnp.where((along == across) & (row_of < lane_of), row_of, -1)
    before = jnp.max(before, axis=0, keepdims=True)
    last = jnp.max(jnp.where(along == lane_of, row_of, -1), axis=0, keepdims=True)
    table = jnp.where(sub_of == 0, before, last)
    tabv[...] = jnp.where(table < 0, TILE, table)
    move = pltpu.make_async_copy(tabv, tabs, t_sem)
    move.start()
    move.wait()
    acc[TILE] = jnp.zeros((MOST, TILE), F32)

    def entry(r, s):
        return jnp.clip(tabs[r, s], 0, TILE)

    def gather(chunk):
        rows = chunk.rows

        def add(d):
            for k in range(SLOTS):
                s = d * 8 + k
                acc[s, :rows] = recv[chunk.slot(d, k)] + acc[entry(0, s), :rows]

        def one(d, _):
            plane_copy(chunk, d, column(1)).wait_recv()
            add(d)
            return 0

        add(0)
        lax.fori_loop(1, PLANE, one, 0)
        for dy in Y_ORDER:
            group = lax.rem(y + dy, SIDE) * 2
            for j in range(OWNED):
                csend[chunk.one(dy, j)] = acc[entry(1, (group + 1 - core) * OWNED + j), :rows]
            core_copy(chunk, dy).start()
        for dy in Y_ORDER:
            group = lax.rem(y + dy, SIDE) * 2
            for j in range(OWNED):
                ysend[chunk.one(dy, j)] = acc[entry(1, (group + core) * OWNED + j), :rows]

    def spread(chunk):
        for dy in Y_ORDER:
            part = chunk.eight(dy)
            core_copy(chunk, dy).wait_recv()
            ysend[part] = ysend[part] + crecv[part]
            if dy:
                y_copy(chunk, dy).start()

    def drain(chunk):
        def one(d, _):
            plane_copy(chunk, d, column(1)).wait_send()
            return 0

        lax.fori_loop(1, PLANE, one, 0)
        for dy in range(SIDE):
            core_copy(chunk, dy).wait_send()
            if dy:
                y_copy(chunk, dy).wait_send()

    def total(chunk):
        for dy in range(1, SIDE):
            y_copy(chunk, dy).wait_recv()
        a, b, c, d = (chunk.eight(dy) for dy in range(SIDE))
        return (ysend[a] + yrecv[b]) + (yrecv[c] + yrecv[d])

    def weights(chunk):
        gather(chunk)
        spread(chunk)

    def sums(chunk):
        value = total(chunk) + 1.0
        for j in range(OWNED):
            block = value[j * chunk.rows:(j + 1) * chunk.rows]
            res[j, pl.ds(chunk.start, chunk.rows), :] = block

    def finish(chunk):
        value = total(chunk)
        for j in range(OWNED):
            part = (j, pl.ds(chunk.start, chunk.rows), slice(None))
            res[part] = value[j * chunk.rows:(j + 1) * chunk.rows] / res[part]

    loop(*weight_args, 0, weights)
    loop(*weight_args, 0, sums)
    loop(*weight_args, 0, drain)

    pixel_chunks = []
    c = WEIGHT_CHUNKS
    for start, rows, count in PIXEL_GROUPS:
        for q in range(count):
            pixel_chunks.append(Chunk(c, start + q * rows, rows, TILE))
            c += 1
    undrained = []
    for index, chunk in enumerate(pixel_chunks):
        gather(chunk)
        spread(chunk)
        if index:
            finish(pixel_chunks[index - 1])
        if index + 1 == len(pixel_chunks):
            break
        undrained.append(chunk)
        if index > 1 and index + 2 < len(pixel_chunks):
            drain(undrained.pop(0))
    finish(pixel_chunks[-1])
    for chunk in undrained + pixel_chunks[-1:]:
        drain(chunk)


def shards(image, weight, coeffs, trim, destination, row_taps, col_taps):
    smem = pl.BlockSpec(memory_space=pltpu.SMEM)
    hbm = pl.BlockSpec(memory_space=pl.ANY)
    dma = pltpu.SemaphoreType.DMA
    stack = 2 * TILE * SIDE * OWNED
    return pl.pallas_call(
        kernel,
        out_shape=pltpu.VMEM((OWNED, TILE, TILE), F32),
        in_specs=[smem] * 5 + [hbm] * 2,
        out_specs=pl.BlockSpec(memory_space=pltpu.VMEM),
        scratch_shapes=[
            pltpu.VMEM((COUNT, TILE, TILE), F32),
            pltpu.VMEM((COUNT, TILE, TILE), F32),
            pltpu.VMEM((COUNT + 1, TILE, TILE), F32),
            pltpu.VMEM((COUNT + 1, TILE, TILE), F32),
            pltpu.VMEM((2, NB * TILE // 2, 2 * TILE), BF16),
            pltpu.VMEM((NB * TILE, 2 * TILE), BF16),
            pltpu.VMEM((2, 2 * TILE, 2 * TILE), BF16),
            pltpu.VMEM((2 * QUAD * TILE, NB * TILE), BF16),
            pltpu.VMEM((PLANE, 2 * TILE * SLOTS, TILE), F32),
            pltpu.VMEM((PLANE, 2 * TILE * SLOTS, TILE), F32),
            pltpu.VMEM((TILE + 1, MOST, TILE), F32),
            pltpu.VMEM((PLANE, 8, TILE), I32),
            pltpu.VMEM((PLANE, 8, TILE), I32),
            pltpu.VMEM((8, TILE), I32),
            pltpu.SMEM((8, TILE), I32),
            pltpu.VMEM((8, TILE), I32),
            pltpu.SMEM((8, TILE), I32),
            pltpu.VMEM((stack, TILE), F32),
            pltpu.VMEM((stack, TILE), F32),
            pltpu.VMEM((stack, TILE), F32),
            pltpu.VMEM((stack, TILE), F32),
            dma(()),
            dma((WEIGHT_CHUNKS,)),
            dma((CHUNKS, PLANE)),
            dma((CHUNKS, PLANE)),
            dma((PLANE,)),
            dma((PLANE,)),
            dma((CHUNKS, SIDE)),
            dma((CHUNKS, SIDE)),
            dma((CHUNKS, SIDE)),
            dma((CHUNKS, SIDE)),
            dma(()),
        ],
        compiler_params=pltpu.CompilerParams(
            collective_id=0, has_side_effects=True, vmem_limit_bytes=60 << 20
        ),
        name="coadd",
    )(destination, trim.T, coeffs.T, row_taps, col_taps, image, weight)


def solution(mesh):
    placed = (
        P(("visit", "patch"), None, None),
        P(("visit", "patch"), None, None),
        P(("visit", "patch"), None),
        P(("visit", "patch"), None),
        P(("visit", "patch")),
        P(),
        P(),
    )
    return jax.shard_map(
        shards,
        mesh=mesh,
        in_specs=placed,
        out_specs=P(("visit", "patch"), None, None),
        check_vma=False,
    )
```
